256 devices in a mesh: freq: 16 (over x, y_hi, core), src: 16 (over y_lo, z).
Axes of the slice: x: 4, y: 4 (y_hi: 2, y_lo: 2; y = y_hi * 2 + y_lo), z: 8, core: 2. Of those that a mesh axis runs over, the one named last changes fastest.
Arguments:
- response: bfloat16 [2, 32, 4096, 4096], P(None, 'freq', 'src'), may hold values from -0.09375 to 0.09375
- focus_plus: bfloat16 [192, 256, 4096], P('freq', None, 'src'), may hold values from -6 to 6
- onset: int32 [192, 4096], P('freq', 'src'), may hold values from 64 to 255
Outputs:
- focus_minus: bfloat16 [192, 256, 4096], P('freq', None, 'src')
The draws below stay inside these ranges and needn't reach their ends.
Inputs may be any that keep to these rules, and one draw needn't show every extreme that they name: onset[x, s] is the first time sample of the direct arrival from position s to focal point x.
All inputs are finite; a program needn't handle non-finite values.
Results may differ from the reference program's by a relative error of at most 0.0066.
Values may be sent and summed in bfloat16 or wider, within the bound.
A program may use at most 128 MiB of HBM per device.

```python
import math
import jax
import jax.numpy as jnp
from jax import lax

NR = 4096
NT = 256
NF = 32
FOC = 192


def set_ends(entries, stream_key, smallest, top_value):
    longest = entries.shape.index(max(entries.shape))
    spots = []
    for shift in (0, 1):
        where = [jax.random.randint(jax.random.fold_in(stream_key, axis), (), 0, length) for axis, length in enumerate(entries.shape)]
        where[longest] = (where[longest] + shift) % entries.shape[longest]
        spots.append(tuple(where))
    return entries.at[spots[0]].set(smallest).at[spots[1]].set(top_value)


def shard_levels(key, extent, cuts, least, largest):
    def one(dim, parts):
        draws = jax.random.uniform(jax.random.fold_in(jax.random.fold_in(key, 6), dim), (parts,), jnp.float32, least / len(cuts), largest / len(cuts))
        return jnp.repeat(jnp.exp(draws), extent[dim] // parts).reshape((-1,) + (1,) * (len(extent) - dim - 1))

    level = one(*cuts[0])
    for cut in cuts[1:]:
        level = level * one(*cut)
    return level


def bell_draw(own_key, extent, deviation, most, pieces=(), kind=jnp.bfloat16):
    level = shard_levels(own_key, extent, pieces, -0.22, 0.18) if pieces else 1.0
    drawn = jax.random.normal(own_key, extent, jnp.float32) * deviation * level
    return jnp.minimum(jnp.maximum(drawn, -most), most).astype(kind)


def setup_inputs(seed: int = 0) -> dict:
    seeds = jax.random.split(jax.random.key(seed), 4)
    return {
        "response": bell_draw(seeds[0], (2, NF, NR, NR), NR ** -0.5, 0.09375, ((1, 16), (2, 16))),
        "focus_plus": bell_draw(seeds[1], (FOC, NT, NR), 1.0, 6.0, ((0, 16), (2, 16))),
        "onset": set_ends(jax.random.randint(seeds[2], (FOC, NR), NT // 4, NT), jax.random.fold_in(seeds[2], 1), NT // 4, NT - 1).astype(jnp.int32),
    }


def phase_angle(first, count, samples):
    bins = first + jnp.arange(count, dtype=jnp.int32) + 1
    times = jnp.arange(samples, dtype=jnp.int32)
    phase = (times[:, None] * bins[None, :]) % samples
    return 2.0 * math.pi * phase.astype(jnp.float32) / samples


def forward_table(first, count, samples):
    angle = phase_angle(first, count, samples)
    return jnp.stack([jnp.cos(angle), -jnp.sin(angle)]).astype(jnp.bfloat16)


def inverse_table(count, samples):
    angle = jnp.transpose(phase_angle(0, count, samples))
    scale = 2.0 / samples
    return jnp.stack([scale * jnp.cos(angle), -scale * jnp.sin(angle)]).astype(jnp.bfloat16)


def reference(response, focus_plus, onset):
    nbin = response.shape[1]
    table = forward_table(0, nbin, NT).astype(jnp.float32)
    spectrum = jnp.einsum("xtr,ctj->cjxr", focus_plus.astype(jnp.float32), table).astype(jnp.bfloat16)

    def one_bin(index):
        real_r = response[0, index]
        imag_r = response[1, index]
        real_f = spectrum[0, index]
        imag_f = spectrum[1, index]
        rr = jnp.dot(real_f, real_r.T, preferred_element_type=jnp.float32)
        ii = jnp.dot(imag_f, imag_r.T, preferred_element_type=jnp.float32)
        ri = jnp.dot(imag_f, real_r.T, preferred_element_type=jnp.float32)
        ir = jnp.dot(real_f, imag_r.T, preferred_element_type=jnp.float32)
        return jnp.stack([rr - ii, ri + ir]).astype(jnp.bfloat16)

    convolved = lax.map(one_bin, jnp.arange(nbin, dtype=jnp.int32))
    convolved = jnp.transpose(convolved, (1, 0, 2, 3))
    inverse = inverse_table(nbin, NT).astype(jnp.float32)
    trace = jnp.einsum("cjxs,cjt->xts", convolved.astype(jnp.float32), inverse)
    times = jnp.arange(NT, dtype=jnp.int32)
    keep = times[None, :, None] < onset[:, None, :]
    return jnp.where(keep, trace, 0.0).astype(jnp.bfloat16)
```

```python
import math

import jax
import jax.numpy as jnp
from jax import lax
from jax.sharding import PartitionSpec as P


def phase_angle(first, count, samples):
    bins = first + jnp.arange(count, dtype=jnp.int32) + 1
    times = jnp.arange(samples, dtype=jnp.int32)
    phase = times[:, None] * bins[None, :] % samples
    return 2.0 * math.pi * phase.astype(jnp.float32) / samples


def forward_table(first, count, samples):
    angle = phase_angle(first, count, samples)
    return jnp.stack([jnp.cos(angle), -jnp.sin(angle)]).astype(jnp.bfloat16)


def inverse_table(count, samples):
    angle = jnp.transpose(phase_angle(0, count, samples))
    scale = 2.0 / samples
    return jnp.stack([scale * jnp.cos(angle), -scale * jnp.sin(angle)]).astype(jnp.bfloat16)


def body(response, focus_plus, onset):
    groups = lax.axis_size("freq")
    per_group = response.shape[1]
    nbin = per_group * groups
    samples = focus_plus.shape[1]
    table = forward_table(0, nbin, samples)
    local = jnp.einsum(
        "xtr,ctj->cjxr", focus_plus, table, preferred_element_type=jnp.float32
    ).astype(jnp.bfloat16)
    local = lax.all_to_all(local, "freq", split_axis=1, concat_axis=2, tiled=True)
    piece = lax.all_gather(local, "src", axis=3, tiled=True)
    real_r = response[0]
    imag_r = response[1]
    real_f = piece[0]
    imag_f = piece[1]
    rr = jnp.einsum("bsr,bxr->bxs", real_r, real_f, preferred_element_type=jnp.float32)
    ii = jnp.einsum("bsr,bxr->bxs", imag_r, imag_f, preferred_element_type=jnp.float32)
    ri = jnp.einsum("bsr,bxr->bxs", real_r, imag_f, preferred_element_type=jnp.float32)
    ir = jnp.einsum("bsr,bxr->bxs", imag_r, real_f, preferred_element_type=jnp.float32)
    real_g = rr - ii
    imag_g = ri + ir
    convolved = jnp.stack([real_g, imag_g]).astype(jnp.bfloat16)
    inverse = inverse_table(nbin, samples)
    trace = jnp.einsum(
        "cjxs,cjt->xts",
        lax.all_to_all(convolved, "freq", split_axis=2, concat_axis=1, tiled=True),
        inverse,
        preferred_element_type=jnp.float32,
    )
    times = jnp.arange(samples, dtype=jnp.int32)
    keep = times[None, :, None] < onset[:, None, :]
    return jnp.where(keep, trace, 0.0).astype(jnp.bfloat16)


def solution(mesh):
    return jax.shard_map(
        body,
        mesh=mesh,
        in_specs=(P(None, "freq", "src", None), P("freq", None, "src"), P("freq", "src")),
        out_specs=P("freq", None, "src"),
        check_vma=False,
    )
```

```python
import math

import jax
import jax.numpy as jnp
import ml_dtypes
import numpy as np
from jax import lax
from jax.experimental import pallas as pl
from jax.experimental.pallas import tpu as pltpu
from jax.sharding import PartitionSpec as P

MESH = pl.DeviceIdType.MESH

NX = 4
NH = 2
NZ = 8
CHIPS = NX * NH
NJ = 2
FOCAL = 12
PAIR = 2 * FOCAL
BLOCK = 2 * PAIR
ROWS = CHIPS * BLOCK
HALF = CHIPS * NJ * 2
NT = 256
LANES = 128
WIDTH = 256
PLACES = ((0, 0), (1, 0), (3, 0), (0, 1), (2, 0), (1, 1), (3, 1), (2, 1))
ROWS_A = 3 * BLOCK


def tables():
    samples = np.arange(NT, dtype=np.int32)
    core, owner, chip, bins, part = np.meshgrid(
        np.arange(2), np.arange(2), np.arange(CHIPS), np.arange(NJ), np.arange(2), indexing="ij"
    )
    index = 4 * chip + 2 * (core ^ owner) + bins + 1
    index = index.reshape(2, 2 * HALF)
    part = part.reshape(2, 2 * HALF)
    phase = (index[..., None] * samples) % NT
    angle = (np.float32(2.0 * math.pi) * phase.astype(np.float32) / np.float32(NT)).astype(np.float32)
    wave = np.where(part[..., None] == 0, np.cos(angle), -np.sin(angle)).astype(np.float32)
    forward = wave.astype(ml_dtypes.bfloat16)
    inverse = (np.float32(2.0 / NT) * wave).astype(ml_dtypes.bfloat16)
    return forward, np.ascontiguousarray(inverse.transpose(0, 2, 1))


def gather_kernel(
    resp_hbm, focus_hbm, table_ref, out_ref,
    resp, focus, mine, pair_out, pair_in, blocks, gath, acc, back_out, back_in, last_out, last_in,
    load_sem, pair_s, pair_r, fwd_s, fwd_r, a_s, a_r, z_s, z_r, y_s, y_r, inv_s, inv_r, last_s, last_r,
):
    f = lax.axis_index("freq")
    me = lax.axis_index("src")
    core = f % 2
    yh = (f // 2) % 2
    x = f // 4
    chip = f // 2
    y = me // NZ
    z = me % NZ
    sibling = (f + 1 - 2 * core, me)
    partner = (1 - y) * NZ + z
    up = (f, y * NZ + (z + 1) % NZ)
    down = (f, y * NZ + (z + NZ - 1) % NZ)
    across = (f, partner)

    def chip_at(dx, dy):
        return ((x + dx) % NX) * NH + (yh + dy) % NH

    ahead = [chip_at(dx, dy) for dx, dy in PLACES]
    behind = [chip_at(NX - dx, dy) for dx, dy in PLACES]

    load_focus = pltpu.make_async_copy(focus_hbm, focus, load_sem.at[0])
    load_focus.start()
    barrier = pltpu.get_barrier_semaphore()
    for peer in [sibling, up, down, across] + [(2 * c + core, me) for c in ahead[1:]]:
        pl.semaphore_signal(barrier, inc=1, device_id=peer, device_id_type=MESH)
    load_focus.wait()
    load_resp = pltpu.make_async_copy(resp_hbm, resp, load_sem.at[1])
    load_resp.start()

    def put(i, rows):
        for h in range(2):
            mine[h, pl.ds(i, HALF, stride=PAIR), :] = rows[:, h * LANES : (h + 1) * LANES]

    def take(i):
        halves = [mine[h, pl.ds(i, HALF, stride=PAIR), :] for h in range(2)]
        return jnp.concatenate(halves, axis=1).astype(jnp.bfloat16)

    def transform(i, _):
        res = jnp.dot(table_ref[core], focus[i], preferred_element_type=jnp.float32)
        put(core * FOCAL + i, res[:HALF])
        pair_out[i] = res[HALF:].astype(jnp.bfloat16)
        return 0

    lax.fori_loop(0, FOCAL, transform, 0)
    acc[...] = jnp.zeros_like(acc)
    pl.semaphore_wait(barrier, 4 + len(PLACES) - 1)
    swap = pltpu.make_async_remote_copy(
        src_ref=pair_out, dst_ref=pair_in, send_sem=pair_s.at[0], recv_sem=pair_r.at[0],
        device_id=sibling, device_id_type=MESH,
    )
    swap.start()
    swap.wait_recv()

    def place(i, _):
        put((1 - core) * FOCAL + i, pair_in[i].astype(jnp.float32))
        return 0

    lax.fori_loop(0, FOCAL, place, 0)
    for h in range(2):
        blocks[:, :, :, pl.ds(h * LANES, LANES)] = mine[h].astype(jnp.bfloat16).reshape(CHIPS, NJ, BLOCK, LANES)

    def forward_copy(p):
        rows = pl.ds(p * BLOCK, BLOCK)
        return pltpu.make_async_remote_copy(
            src_ref=blocks.at[behind[p]], dst_ref=gath.at[:, me, rows],
            send_sem=fwd_s.at[p], recv_sem=fwd_r.at[p],
            device_id=(2 * behind[p] + core, me), device_id_type=MESH,
        )

    for p in range(1, len(PLACES)):
        forward_copy(p).start()
    gath[:, me, :BLOCK, :] = blocks[chip]

    part_a = (0, ROWS_A)
    part_b = (ROWS_A, ROWS - ROWS_A)
    spans = (part_b, part_a, part_a)
    rings = (up, down)

    def z_copy(d, t, s, o):
        block = gath.at[d, o, pl.ds(*spans[t])]
        return pltpu.make_async_remote_copy(
            src_ref=block, dst_ref=block, send_sem=z_s.at[d, t, s], recv_sem=z_r.at[d, t, s],
            device_id=rings[d], device_id_type=MESH,
        )

    def y_copy(d, s, o):
        block = gath.at[d, o, pl.ds(*part_b)]
        return pltpu.make_async_remote_copy(
            src_ref=block, dst_ref=block, send_sem=y_s.at[d, s], recv_sem=y_r.at[d, s],
            device_id=across, device_id_type=MESH,
        )

    def a_copy(o):
        block = gath.at[:, o, pl.ds(*part_a)]
        return pltpu.make_async_remote_copy(
            src_ref=block, dst_ref=block, send_sem=a_s.at[0], recv_sem=a_r.at[0],
            device_id=across, device_id_type=MESH,
        )

    def products(d, o, span):
        rows = pl.ds(*span)
        piece = gath[d, o, rows, :]
        columns = pl.ds(pl.multiple_of(o * WIDTH, WIDTH), WIDTH)
        for c in range(2):
            acc[d, c, rows, :] += lax.dot_general(
                piece, resp[c, d, :, columns], (((1,), (1,)), ((), ())),
                preferred_element_type=jnp.float32,
            )

    def at(d, s):
        return (z + NZ - s) % NZ if d == 0 else (z + s) % NZ

    for p in (1, 2):
        forward_copy(p).wait_recv()
    a_copy(me).start()
    for d in range(NJ):
        z_copy(d, 1, 0, me).start()
    for p in range(3, len(PLACES)):
        forward_copy(p).wait_recv()
    for d in range(NJ):
        z_copy(d, 0, 0, me).start()
        y_copy(d, 0, me).start()
    load_resp.wait()
    for d in range(NJ):
        products(d, me, part_a)
    a_copy(partner).wait_recv()
    for d in range(NJ):
        z_copy(d, 2, 0, partner).start()
    for d in range(NJ):
        products(d, me, part_b)
        products(d, partner, part_a)

    def step(s, _):
        for t in range(3):
            for d in range(NJ):
                o = (y if t < 2 else 1 - y) * NZ + at(d, s + 1)
                z_copy(d, t, s, o).wait_recv()

                @pl.when(s < NZ - 2)
                def _():
                    z_copy(d, t, s + 1, o).start()

                if t == 0:
                    y_copy(d, s + 1, o).start()
                products(d, o, spans[t])
        for d in range(NJ):
            o = (1 - y) * NZ + at(d, s)
            y_copy(d, s, o).wait_recv()
            products(d, o, part_b)
        return 0

    lax.fori_loop(0, NZ - 1, step, 0)
    for d in range(NJ):
        o = (1 - y) * NZ + at(d, NZ - 1)
        y_copy(d, NZ - 1, o).wait_recv()
        products(d, o, part_b)

    def back_copy(p):
        return pltpu.make_async_remote_copy(
            src_ref=back_out.at[p], dst_ref=back_in.at[chip],
            send_sem=inv_s.at[p], recv_sem=inv_r.at[p],
            device_id=(2 * ahead[p] + core, me), device_id_type=MESH,
        )

    for p in range(len(PLACES) - 1, -1, -1):
        for d in range(NJ):
            start = p * BLOCK
            re = acc[d, 0, start : start + PAIR, :] - acc[d, 1, start + PAIR : start + BLOCK, :]
            im = acc[d, 0, start + PAIR : start + BLOCK, :] + acc[d, 1, start : start + PAIR, :]
            both = jnp.concatenate([re, im], axis=0).astype(jnp.bfloat16)
            if p == 0:
                back_in[chip, d] = both
            else:
                back_out[p, d] = both
        if p > 0:
            back_copy(p).start()
    for p in range(1, len(PLACES)):
        back_copy(p).wait_recv()
    for h in range(2):
        mine[h] = back_in[:, :, :, pl.ds(h * LANES, LANES)].astype(jnp.float32).reshape(HALF * PAIR, LANES)

    def theirs(i, _):
        last_out[i] = take((1 - core) * FOCAL + i)
        return 0

    lax.fori_loop(0, FOCAL, theirs, 0)
    last = pltpu.make_async_remote_copy(
        src_ref=last_out, dst_ref=last_in, send_sem=last_s.at[0], recv_sem=last_r.at[0],
        device_id=sibling, device_id_type=MESH,
    )
    last.start()

    def own(i, _):
        out_ref[i, :HALF, :] = take(core * FOCAL + i)
        return 0

    lax.fori_loop(0, FOCAL, own, 0)
    last.wait_recv()
    out_ref[:, HALF:, :] = last_in[...]

    last.wait_send()
    swap.wait_send()
    a_copy(me).wait_send()
    for p in range(1, len(PLACES)):
        forward_copy(p).wait_send()
        back_copy(p).wait_send()

    def drain(s, _):
        for d in range(NJ):
            for t in range(3):
                z_copy(d, t, s, me).wait_send()
            y_copy(d, s, me).wait_send()
        return 0

    lax.fori_loop(0, NZ - 1, drain, 0)
    for d in range(NJ):
        y_copy(d, NZ - 1, me).wait_send()


def gather(response, focus_plus, table):
    bf16 = jnp.bfloat16
    dma = pltpu.SemaphoreType.DMA
    places = len(PLACES)
    return pl.pallas_call(
        gather_kernel,
        out_shape=jax.ShapeDtypeStruct((FOCAL, 2 * HALF, WIDTH), bf16),
        in_specs=[
            pl.BlockSpec(memory_space=pl.ANY),
            pl.BlockSpec(memory_space=pl.ANY),
            pl.BlockSpec(memory_space=pltpu.VMEM),
        ],
        out_specs=pl.BlockSpec(memory_space=pltpu.VMEM),
        scratch_shapes=[
            pltpu.VMEM(response.shape, bf16),
            pltpu.VMEM(focus_plus.shape, bf16),
            pltpu.VMEM((2, HALF * PAIR, LANES), jnp.float32),
            pltpu.VMEM((FOCAL, HALF, WIDTH), bf16),
            pltpu.VMEM((FOCAL, HALF, WIDTH), bf16),
            pltpu.VMEM((CHIPS, NJ, BLOCK, WIDTH), bf16),
            pltpu.VMEM((NJ, 2 * NZ, ROWS, WIDTH), bf16),
            pltpu.VMEM((NJ, 2, ROWS, WIDTH), jnp.float32),
            pltpu.VMEM((CHIPS, NJ, BLOCK, WIDTH), bf16),
            pltpu.VMEM((CHIPS, NJ, BLOCK, WIDTH), bf16),
            pltpu.VMEM((FOCAL, HALF, WIDTH), bf16),
            pltpu.VMEM((FOCAL, HALF, WIDTH), bf16),
            dma((2,)),
            dma((1,)), dma((1,)),
            dma((places,)), dma((places,)),
            dma((1,)), dma((1,)),
            dma((NJ, 3, NZ - 1)), dma((NJ, 3, NZ - 1)),
            dma((NJ, NZ)), dma((NJ, NZ)),
            dma((places,)), dma((places,)),
            dma((1,)), dma((1,)),
        ],
        compiler_params=pltpu.CompilerParams(
            collective_id=0, has_side_effects=True, vmem_limit_bytes=40 << 20
        ),
        name="gather",
    )(response, focus_plus, table)


GROUP = 3


def inverse_kernel(spectra_ref, table_ref, onset_ref, out_ref):
    core = lax.axis_index("freq") % 2
    table = table_ref[core]
    times = lax.broadcasted_iota(jnp.int32, (NT, WIDTH), 0)
    first = pl.program_id(0) * GROUP
    for i in range(GROUP):
        trace = jnp.dot(table, spectra_ref[i], preferred_element_type=jnp.float32)
        onset = onset_ref[pl.ds(first + i, 1), :]
        out_ref[i] = jnp.where(times < onset, trace, 0.0).astype(jnp.bfloat16)


def inverse(spectra, table, onset):
    return pl.pallas_call(
        inverse_kernel,
        grid=(FOCAL // GROUP,),
        out_shape=jax.ShapeDtypeStruct((FOCAL, NT, WIDTH), jnp.bfloat16),
        in_specs=[
            pl.BlockSpec((GROUP, 2 * HALF, WIDTH), lambda i: (i, 0, 0)),
            pl.BlockSpec((2, NT, 2 * HALF), lambda i: (0, 0, 0)),
            pl.BlockSpec((FOCAL, WIDTH), lambda i: (0, 0)),
        ],
        out_specs=pl.BlockSpec((GROUP, NT, WIDTH), lambda i: (i, 0, 0)),
        name="inverse",
    )(spectra, table, onset)


def body(response, focus_plus, onset):
    forward_table, inverse_table = tables()
    spectra = gather(response, focus_plus, jnp.asarray(forward_table))
    return inverse(spectra, jnp.asarray(inverse_table), onset)


def solution(mesh):
    return jax.shard_map(
        body,
        mesh=mesh,
        in_specs=(P(None, "freq", "src", None), P("freq", None, "src"), P("freq", "src")),
        out_specs=P("freq", None, "src"),
        check_vma=False,
    )
```

```python
import functools
import math

import jax
import jax.numpy as jnp
import ml_dtypes
import numpy as np
from jax import lax
from jax.experimental import pallas as pl
from jax.experimental.pallas import tpu as pltpu
from jax.sharding import PartitionSpec as P

MESH = pl.DeviceIdType.MESH

NX = 4
NH = 2
NZ = 8
CHIPS = NX * NH
PEERS = 2 * CHIPS
NJ = 2
FOCAL = 12
GROUPS = 3
FEW = FOCAL // GROUPS
TILE = NJ * 2 * FEW
PIECE = 2 * FEW
ROWS = PEERS * PIECE
HALF = NJ * 2 * PEERS
NT = 256
LANES = 128
WIDTH = 256
FAR = NZ // 2
CHIP_PLACES = ((0, 0), (1, 0), (3, 0), (0, 1), (2, 0), (1, 1), (3, 1), (2, 1))
PLACES = tuple((dx, dy, dc) for dx, dy in CHIP_PLACES for dc in range(2))
BATCHES = ((0, 1), (1, 1), (2, 1))
PLACES_A = (3, 3, 4)
STARTS = (0.0, 0.2, 0.4)
LEADS = (1.5, 0.5)
LAG = 1.05


def tables():
    samples = np.arange(NT, dtype=np.int32)
    bins = (np.arange(HALF) // 2 + 1).astype(np.int32)
    part = np.arange(HALF) % 2
    phase = (bins[:, None] * samples) % NT
    angle = (np.float32(2.0 * math.pi) * phase.astype(np.float32) / np.float32(NT)).astype(np.float32)
    wave = np.where(part[:, None] == 0, np.cos(angle), -np.sin(angle)).astype(np.float32)
    inverse = np.float32(2.0 / NT) * wave
    return wave.astype(ml_dtypes.bfloat16), np.ascontiguousarray(inverse.T).astype(ml_dtypes.bfloat16)


def gather_kernel(
    resp_hbm, focus_hbm, table_hbm, out_hbm,
    resp, focus, table, mine, blocks, arrived, gath, acc, back_out,
    load_sem, own_sem, fwd_s, fwd_r, a_s, a_r, z_s, z_r, y_s, y_r, inv_s, inv_r,
):
    f = lax.axis_index("freq")
    me = lax.axis_index("src")
    core = f % 2
    yh = (f // 2) % 2
    x = f // 4
    y = me // NZ
    z = me % NZ
    partner = (1 - y) * NZ + z
    rings = ((f, y * NZ + (z + 1) % NZ), (f, y * NZ + (z + NZ - 1) % NZ))
    across = (f, partner)

    def device_at(dx, dy, dc):
        return (((x + dx) % NX) * NH + (yh + dy) % NH) * 2 + (core + dc) % 2

    ahead = [device_at(*place) for place in PLACES]
    behind = [device_at(NX - dx, dy, dc) for dx, dy, dc in PLACES]
    batches = range(len(BATCHES))

    def few(ref, g):
        return ref.at[pl.ds(g * FEW, FEW)]

    def load_focus(g):
        return pltpu.make_async_copy(few(focus_hbm, g), few(focus, g), load_sem.at[g])

    load_table = pltpu.make_async_copy(table_hbm, table, load_sem.at[GROUPS])
    load_resp = pltpu.make_async_copy(resp_hbm, resp, load_sem.at[GROUPS + 1])
    load_table.start()
    for g in range(GROUPS):
        load_focus(g).start()
    barrier = pltpu.get_barrier_semaphore()
    peers = [*rings, across] + [(d, me) for d in ahead[1:]]
    for peer in peers:
        pl.semaphore_signal(barrier, inc=1, device_id=peer, device_id_type=MESH)

    def transform(g):
        load_focus(g).wait()
        waves = table[...]

        def one(i, _):
            res = jnp.dot(waves, focus[g * FEW + i], preferred_element_type=jnp.float32)
            for h in range(2):
                mine[g, h, pl.ds(i, HALF, stride=FEW), :] = res[:, h * LANES : (h + 1) * LANES]
            return 0

        lax.fori_loop(0, FEW, one, 0)
        for h in range(2):
            rows = mine[g, h].astype(jnp.bfloat16).reshape(PEERS, TILE, LANES)
            blocks[g, :, :, pl.ds(h * LANES, LANES)] = rows

    def groups_of(b):
        return pl.ds(*BATCHES[b])

    def forward_copy(b, q):
        return pltpu.make_async_remote_copy(
            src_ref=blocks.at[groups_of(b), behind[q]], dst_ref=arrived.at[groups_of(b), q],
            send_sem=fwd_s.at[b, q], recv_sem=fwd_r.at[b, q],
            device_id=(behind[q], me), device_id_type=MESH,
        )

    def spread(b):
        for q in range(1, PEERS):
            forward_copy(b, q).start()
        first, count = BATCHES[b]
        for g in range(first, first + count):
            arrived[g, 0] = blocks[g, f]

    def collect(b, first_chip, last_chip):
        for q in range(max(1, 2 * first_chip), 2 * last_chip):
            forward_copy(b, q).wait_recv()
        first, count = BATCHES[b]
        for g in range(first, first + count):
            for p in range(first_chip, last_chip):
                both = [arrived[g, 2 * p + c].astype(jnp.float32) for c in range(2)]
                for j in range(NJ):
                    rows = [tile[j * PIECE : (j + 1) * PIECE] for tile in both]
                    gath[j, me, g, p] = jnp.concatenate(rows, axis=0).astype(jnp.bfloat16)

    def span(b, t):
        return pl.ds(0, PLACES_A[b]) if t else pl.ds(PLACES_A[b], CHIPS - PLACES_A[b])

    def owner(d, r, column):
        return column * NZ + ((z + 2 * NZ - 1 - r) % NZ if d == 0 else (z + 1 + r) % NZ)

    def piece(b, d, r, o, places):
        if r < FAR - 1:
            return gath.at[:, o, groups_of(b), places]
        return gath.at[d, o, groups_of(b), places]

    def z_copy(d, t, b, r, o):
        block = piece(b, d, r, o, span(b, t))
        return pltpu.make_async_remote_copy(
            src_ref=block, dst_ref=block, send_sem=z_s.at[d, t, b, r], recv_sem=z_r.at[d, t, b, r],
            device_id=rings[d], device_id_type=MESH,
        )

    def z_send(d, t, b, r):
        return z_copy(d, t, b, r, owner(d, r - 1, 1 - y if t == 2 else y))

    def z_recv(d, t, b, r):
        return z_copy(d, t, b, r, owner(d, r, 1 - y if t == 2 else y))

    def y_copy(d, b, r, column):
        block = piece(b, d, r, owner(d, r, column), span(b, 0))
        return pltpu.make_async_remote_copy(
            src_ref=block, dst_ref=block, send_sem=y_s.at[d, b, r + 1], recv_sem=y_r.at[d, b, r + 1],
            device_id=across, device_id_type=MESH,
        )

    def a_copy(b, o):
        block = piece(b, 0, -1, o, span(b, 1))
        return pltpu.make_async_remote_copy(
            src_ref=block, dst_ref=block, send_sem=a_s.at[b], recv_sem=a_r.at[b],
            device_id=across, device_id_type=MESH,
        )

    def ways(r):
        return (0,) if r < 0 else (0, 1)

    def products(b, owners, fresh=False):
        first, count = BATCHES[b]
        rows = pl.ds(first * ROWS, count * ROWS)

        def one(d, _):
            for c in range(2):
                total = None
                for o in owners:
                    columns = pl.ds(pl.multiple_of(o * WIDTH, WIDTH), WIDTH)
                    block = gath[d, o, pl.ds(first, count)].reshape(count * ROWS, WIDTH)
                    term = lax.dot_general(
                        block, resp[c, d, :, columns], (((1,), (1,)), ((), ())),
                        preferred_element_type=jnp.float32,
                    )
                    total = term if total is None else total + term
                if fresh:
                    acc[d, c, rows, :] = total
                else:
                    acc[d, c, rows, :] += total
            return 0

        lax.fori_loop(0, NJ, one, 0)

    def begin(b):
        collect(b, 0, PLACES_A[b])
        a_copy(b, me).start()
        for d in range(2):
            z_send(d, 1, b, 0).start()
        collect(b, PLACES_A[b], CHIPS)
        for d in range(2):
            z_send(d, 0, b, 0).start()
        y_copy(0, b, -1, y).start()

    def begin_across(b):
        a_copy(b, partner).wait_recv()
        for d in range(2):
            z_send(d, 2, b, 0).start()
        products(b, [me], fresh=True)

    def owners_at(r, column):
        both = [owner(d, r, column) for d in ways(r)]
        return [partner] if r < 0 else both[:1] if r == FAR - 1 else both

    def step(b, r):
        for t in range(3):
            for d in range(2):
                z_recv(d, t, b, r).wait_recv()
                if r < FAR - 1:
                    z_send(d, t, b, r + 1).start()
                if t == 0:
                    y_copy(d, b, r, y).start()
        products(b, owners_at(r, y))

    def step_across(b, r):
        for d in ways(r):
            y_copy(d, b, r, 1 - y).wait_recv()
        products(b, owners_at(r, 1 - y))

    def back_copy(b, q):
        return pltpu.make_async_remote_copy(
            src_ref=back_out.at[groups_of(b), q], dst_ref=out_hbm.at[groups_of(b), f],
            send_sem=inv_s.at[b, q], recv_sem=inv_r.at[b, q],
            device_id=(ahead[q], me), device_id_type=MESH,
        )

    def keep_own(b):
        return pltpu.make_async_copy(back_out.at[groups_of(b), 0], out_hbm.at[groups_of(b), f], own_sem.at[b])

    def finish(b):
        sign = jnp.where(lax.broadcasted_iota(jnp.int32, (PEERS, PIECE, WIDTH), 1) < FEW, -1.0, 1.0)
        first, count = BATCHES[b]
        for g in range(first, first + count):
            rows = pl.ds(g * ROWS, ROWS)
            bins = []
            for j in range(NJ):
                straight = acc[j, 0, rows, :].reshape(PEERS, PIECE, WIDTH)
                turned = acc[j, 1, rows, :].reshape(PEERS, PIECE, WIDTH)
                bins.append(straight + sign * pltpu.roll(turned, FEW, 1))
            back_out[g] = jnp.concatenate(bins, axis=1).astype(jnp.bfloat16)
        for q in range(PEERS - 1, 0, -1):
            back_copy(b, q).start()
        keep_own(b).start()

    load_table.wait()
    for g in range(GROUPS):
        transform(g)
        if g == 0:
            load_resp.start()
            pl.semaphore_wait(barrier, len(peers))
        for b in batches:
            if sum(BATCHES[b]) == g + 1:
                spread(b)
    begin(0)
    load_resp.wait()
    begin_across(0)

    events = []
    for b in batches:
        if b > 0:
            events.append((STARTS[b] - LEADS[0], b, begin))
            events.append((STARTS[b] - LEADS[1], b, begin_across))
        for r in range(-1, FAR):
            if r >= 0:
                events.append((STARTS[b] + r, b, functools.partial(step, r=r)))
            events.append((STARTS[b] + r + LAG, b, functools.partial(step_across, r=r)))
        events.append((STARTS[b] + FAR - 1 + LAG, b, finish))
    for _, b, event in sorted(events, key=lambda e: e[:2]):
        event(b)

    for b in batches:
        keep_own(b).wait()
        a_copy(b, me).wait_send()
        for q in range(1, PEERS):
            back_copy(b, q).wait_recv()
            forward_copy(b, q).wait_send()
            back_copy(b, q).wait_send()
        for r in range(-1, FAR):
            for d in ways(r):
                y_copy(d, b, r, y).wait_send()
                for t in range(3):
                    if r >= 0:
                        z_send(d, t, b, r).wait_send()


def gather(response, focus_plus, table):
    bf16 = jnp.bfloat16
    dma = pltpu.SemaphoreType.DMA
    hbm = pl.BlockSpec(memory_space=pltpu.HBM)
    parts = len(BATCHES)
    return pl.pallas_call(
        gather_kernel,
        out_shape=jax.ShapeDtypeStruct((GROUPS, PEERS, TILE, WIDTH), bf16),
        in_specs=[hbm] * 3,
        out_specs=hbm,
        scratch_shapes=[
            pltpu.VMEM(response.shape, bf16),
            pltpu.VMEM(focus_plus.shape, bf16),
            pltpu.VMEM(table.shape, bf16),
            pltpu.VMEM((GROUPS, 2, HALF * FEW, LANES), jnp.float32),
            pltpu.VMEM((GROUPS, PEERS, TILE, WIDTH), bf16),
            pltpu.VMEM((GROUPS, PEERS, TILE, WIDTH), bf16),
            pltpu.VMEM((NJ, 2 * NZ, GROUPS, CHIPS, 2 * PIECE, WIDTH), bf16),
            pltpu.VMEM((NJ, 2, GROUPS * ROWS, WIDTH), jnp.float32),
            pltpu.VMEM((GROUPS, PEERS, TILE, WIDTH), bf16),
            dma((GROUPS + 2,)),
            dma((parts,)),
            dma((parts, PEERS)), dma((parts, PEERS)),
            dma((parts,)), dma((parts,)),
            dma((2, 3, parts, FAR)), dma((2, 3, parts, FAR)),
            dma((2, parts, FAR + 1)), dma((2, parts, FAR + 1)),
            dma((parts, PEERS)), dma((parts, PEERS)),
        ],
        compiler_params=pltpu.CompilerParams(
            collective_id=0, has_side_effects=True, vmem_limit_bytes=60 << 20
        ),
        name="gather",
    )(response, focus_plus, table)


def inverse_kernel(spectra_ref, table_ref, onset_ref, out_hbm, mine, out, sem):
    times = lax.broadcasted_iota(jnp.int32, (NT, WIDTH), 0)
    waves = table_ref[...]

    def store(i):
        return pltpu.make_async_copy(out.at[i], out_hbm.at[i], sem.at[i])

    for g in range(GROUPS):
        for h in range(2):
            rows = spectra_ref[g, :, :, pl.ds(h * LANES, LANES)].astype(jnp.float32)
            mine[g, h] = rows.reshape(HALF * FEW, LANES)
        for i in range(FEW):
            halves = [mine[g, h, pl.ds(i, HALF, stride=FEW), :] for h in range(2)]
            spectra = jnp.concatenate(halves, axis=1).astype(jnp.bfloat16)
            trace = jnp.dot(waves, spectra, preferred_element_type=jnp.float32)
            at = g * FEW + i
            out[at] = jnp.where(times < onset_ref[at : at + 1, :], trace, 0.0).astype(jnp.bfloat16)
            store(at).start()
    for i in range(FOCAL):
        store(i).wait()


def inverse(spectra, table, onset):
    vmem = pl.BlockSpec(memory_space=pltpu.VMEM)
    shape = (FOCAL, NT, WIDTH)
    return pl.pallas_call(
        inverse_kernel,
        out_shape=jax.ShapeDtypeStruct(shape, jnp.bfloat16),
        in_specs=[vmem] * 3,
        out_specs=pl.BlockSpec(memory_space=pltpu.HBM),
        scratch_shapes=[
            pltpu.VMEM((GROUPS, 2, HALF * FEW, LANES), jnp.float32),
            pltpu.VMEM(shape, jnp.bfloat16),
            pltpu.SemaphoreType.DMA((FOCAL,)),
        ],
        compiler_params=pltpu.CompilerParams(vmem_limit_bytes=60 << 20),
        name="inverse",
    )(spectra, table, onset)


def body(response, focus_plus, onset):
    forward_table, inverse_table = tables()
    spectra = gather(response, focus_plus, jnp.asarray(forward_table))
    return inverse(spectra, jnp.asarray(inverse_table), onset)


def solution(mesh):
    return jax.shard_map(
        body,
        mesh=mesh,
        in_specs=(P(None, "freq", "src", None), P("freq", None, "src"), P("freq", "src")),
        out_specs=P("freq", None, "src"),
        check_vma=False,
    )
```

```python
import functools
import math

import jax
import jax.numpy as jnp
import ml_dtypes
import numpy as np
from jax import lax
from jax.experimental import pallas as pl
from jax.experimental.pallas import tpu as pltpu
from jax.sharding import PartitionSpec as P

MESH = pl.DeviceIdType.MESH

NX = 4
NH = 2
NZ = 8
CHIPS = NX * NH
PEERS = 2 * CHIPS
NJ = 2
FOCAL = 12
GROUPS = 3
FEW = FOCAL // GROUPS
TILE = NJ * 2 * FEW
PIECE = 2 * FEW
ROWS = PEERS * PIECE
HALF = NJ * 2 * PEERS
TABLE = 1024
NT = 256
LANES = 128
WIDTH = 256
FAR = NZ // 2
CHIP_PLACES = ((0, 0), (1, 0), (3, 0), (0, 1), (2, 0), (1, 1), (3, 1), (2, 1))
PLACES = tuple((dx, dy, dc) for dx, dy in CHIP_PLACES for dc in range(2))
BATCHES = ((0, 3),)
PLACES_A = (3,)
AHEAD = 1.1
STARTS = (0.0,)
LEADS = (1.5, 0.5)
LAG = 1.05
OWN = len(BATCHES)


def tables():
    samples = np.arange(NT, dtype=np.int32)
    bins = (np.arange(TABLE) // 2 + 1).astype(np.int32)
    part = np.arange(TABLE) % 2
    phase = (bins[:, None] * samples) % NT
    angle = (np.float32(2.0 * math.pi) * phase.astype(np.float32) / np.float32(NT)).astype(np.float32)
    wave = np.where(part[:, None] == 0, np.cos(angle), -np.sin(angle)).astype(np.float32)
    inverse = np.float32(2.0 / NT) * wave[:HALF]
    return wave.astype(ml_dtypes.bfloat16), np.ascontiguousarray(inverse.T).astype(ml_dtypes.bfloat16)


def gather_kernel(
    resp_hbm, focus_hbm, table_hbm, out_hbm,
    resp, focus, table, mine, blocks, arrived, gath, acc, back_out,
    load_sem, own_sem, fwd_s, fwd_r, a_s, a_r, z_s, z_r, y_s, y_r, inv_s, inv_r,
):
    f = lax.axis_index("freq")
    me = lax.axis_index("src")
    core = f % 2
    yh = (f // 2) % 2
    x = f // 4
    y = me // NZ
    z = me % NZ
    partner = (1 - y) * NZ + z
    rings = ((f, y * NZ + (z + 1) % NZ), (f, y * NZ + (z + NZ - 1) % NZ))
    across = (f, partner)

    def device_at(dx, dy, dc):
        return (((x + dx) % NX) * NH + (yh + dy) % NH) * 2 + (core + dc) % 2

    ahead = [device_at(*place) for place in PLACES]
    behind = [device_at(NX - dx, dy, dc) for dx, dy, dc in PLACES]
    batches = range(len(BATCHES))

    def few(ref, g):
        return ref.at[pl.ds(g * FEW, FEW)]

    def load_focus(g):
        return pltpu.make_async_copy(few(focus_hbm, g), few(focus, g), load_sem.at[g])

    load_table = pltpu.make_async_copy(table_hbm.at[pl.ds(0, HALF)], table, load_sem.at[GROUPS])
    load_resp = pltpu.make_async_copy(resp_hbm, resp, load_sem.at[GROUPS + 1])
    load_table.start()
    for g in range(GROUPS):
        load_focus(g).start()
    barrier = pltpu.get_barrier_semaphore()
    peers = [*rings, across] + [(d, me) for d in ahead[1:]]
    for peer in peers:
        pl.semaphore_signal(barrier, inc=1, device_id=peer, device_id_type=MESH)

    def transform(g):
        load_focus(g).wait()
        waves = table[...]

        def one(i, _):
            res = jnp.dot(waves, focus[g * FEW + i], preferred_element_type=jnp.float32)
            for h in range(2):
                mine[g, h, pl.ds(i, HALF, stride=FEW), :] = res[:, h * LANES : (h + 1) * LANES]
            return 0

        lax.fori_loop(0, FEW, one, 0)
        for h in range(2):
            rows = mine[g, h].astype(jnp.bfloat16).reshape(PEERS, TILE, LANES)
            blocks[g, :, :, pl.ds(h * LANES, LANES)] = rows

    def groups_of(b):
        return pl.ds(0, GROUPS) if b == OWN else pl.ds(*BATCHES[b])

    def forward_copy(b, q):
        return pltpu.make_async_remote_copy(
            src_ref=blocks.at[groups_of(b), behind[q]], dst_ref=arrived.at[groups_of(b), q],
            send_sem=fwd_s.at[b, q], recv_sem=fwd_r.at[b, q],
            device_id=(behind[q], me), device_id_type=MESH,
        )

    def spread(b):
        for q in range(1, PEERS):
            forward_copy(b, q).start()
        first, count = BATCHES[b]
        for g in range(first, first + count):
            arrived[g, 0] = blocks[g, f]

    def collect(b, first_chip, last_chip):
        for q in range(2 * first_chip, 2 * last_chip):
            if q > 0:
                forward_copy(b, q).wait_recv()
        first, count = BATCHES[b]
        for g in range(first, first + count):
            for p in range(first_chip, last_chip):
                both = [arrived[g, 2 * p + c].astype(jnp.float32) for c in range(2)]
                for j in range(NJ):
                    rows = [tile[j * PIECE : (j + 1) * PIECE] for tile in both]
                    gath[j, me, g, p] = jnp.concatenate(rows, axis=0).astype(jnp.bfloat16)

    def span(b, t):
        if b == OWN:
            return pl.ds(0, 1)
        return pl.ds(1, PLACES_A[b]) if t else pl.ds(1 + PLACES_A[b], CHIPS - 1 - PLACES_A[b])

    def owner(d, r, column):
        return column * NZ + ((z + 2 * NZ - 1 - r) % NZ if d == 0 else (z + 1 + r) % NZ)

    def piece(b, d, r, o, places):
        if r < FAR - 1:
            return gath.at[:, o, groups_of(b), places]
        return gath.at[d, o, groups_of(b), places]

    def z_copy(d, t, b, r, o):
        block = piece(b, d, r, o, span(b, t))
        return pltpu.make_async_remote_copy(
            src_ref=block, dst_ref=block, send_sem=z_s.at[d, t, b, r], recv_sem=z_r.at[d, t, b, r],
            device_id=rings[d], device_id_type=MESH,
        )

    def z_send(d, t, b, r):
        return z_copy(d, t, b, r, owner(d, r - 1, 1 - y if t == 2 else y))

    def z_recv(d, t, b, r):
        return z_copy(d, t, b, r, owner(d, r, 1 - y if t == 2 else y))

    def y_copy(d, b, r, column):
        block = piece(b, d, r, owner(d, r, column), span(b, 0))
        return pltpu.make_async_remote_copy(
            src_ref=block, dst_ref=block, send_sem=y_s.at[d, b, r + 1], recv_sem=y_r.at[d, b, r + 1],
            device_id=across, device_id_type=MESH,
        )

    def a_copy(b, o):
        block = piece(b, 0, -1, o, span(b, 1))
        return pltpu.make_async_remote_copy(
            src_ref=block, dst_ref=block, send_sem=a_s.at[b], recv_sem=a_r.at[b],
            device_id=across, device_id_type=MESH,
        )

    def ways(r):
        return (0,) if r < 0 else (0, 1)

    def products(b, owners, fresh=False):
        first, count = BATCHES[b]
        rows = pl.ds(first * ROWS, count * ROWS)

        def one(d, _):
            for c in range(2):
                total = None
                for o in owners:
                    columns = pl.ds(pl.multiple_of(o * WIDTH, WIDTH), WIDTH)
                    block = gath[d, o, pl.ds(first, count)].reshape(count * ROWS, WIDTH)
                    term = lax.dot_general(
                        block, resp[c, d, :, columns], (((1,), (1,)), ((), ())),
                        preferred_element_type=jnp.float32,
                    )
                    total = term if total is None else total + term
                if fresh:
                    acc[d, c, rows, :] = total
                else:
                    acc[d, c, rows, :] += total
            return 0

        lax.fori_loop(0, NJ, one, 0)

    def begin_chip():
        for b in batches:
            collect(b, 0, 1)
        for d in range(2):
            z_send(d, 0, OWN, 0).start()
        y_copy(0, OWN, -1, y).start()

    def begin(b):
        collect(b, 1, 1 + PLACES_A[b])
        a_copy(b, me).start()
        for d in range(2):
            z_send(d, 1, b, 0).start()
        collect(b, 1 + PLACES_A[b], CHIPS)
        for d in range(2):
            z_send(d, 0, b, 0).start()
        y_copy(0, b, -1, y).start()

    def begin_across(b):
        if b == 0:
            load_resp.wait()
        a_copy(b, partner).wait_recv()
        for d in range(2):
            z_send(d, 2, b, 0).start()
        products(b, [me], fresh=True)

    def owners_at(r, column):
        both = [owner(d, r, column) for d in ways(r)]
        return [partner] if r < 0 else both[:1] if r == FAR - 1 else both

    def step(b, r):
        for t in range(1 if b == OWN else 3):
            for d in range(2):
                z_recv(d, t, b, r).wait_recv()
                if r < FAR - 1:
                    z_send(d, t, b, r + 1).start()
                if t == 0:
                    y_copy(d, b, r, y).start()
        if b != OWN:
            products(b, owners_at(r, y))

    def step_across(b, r):
        for d in ways(r):
            y_copy(d, b, r, 1 - y).wait_recv()
        if b != OWN:
            products(b, owners_at(r, 1 - y))

    def back_copy(b, q):
        return pltpu.make_async_remote_copy(
            src_ref=back_out.at[groups_of(b), q], dst_ref=out_hbm.at[groups_of(b), f],
            send_sem=inv_s.at[b, q], recv_sem=inv_r.at[b, q],
            device_id=(ahead[q], me), device_id_type=MESH,
        )

    def keep_own(b):
        return pltpu.make_async_copy(back_out.at[groups_of(b), 0], out_hbm.at[groups_of(b), f], own_sem.at[b])

    def finish(b):
        sign = jnp.where(lax.broadcasted_iota(jnp.int32, (PIECE, WIDTH), 0) < FEW, -1.0, 1.0)
        first, count = BATCHES[b]
        for q in range(PEERS - 1, -1, -1):
            for g in range(first, first + count):
                rows = pl.ds(g * ROWS + q * PIECE, PIECE)
                bins = [
                    acc[j, 0, rows, :] + sign * pltpu.roll(acc[j, 1, rows, :], FEW, 0) for j in range(NJ)
                ]
                back_out[g, q] = jnp.concatenate(bins, axis=0).astype(jnp.bfloat16)
            if q > 0:
                back_copy(b, q).start()
            else:
                keep_own(b).start()

    load_table.wait()
    for g in range(GROUPS):
        transform(g)
        if g == 0:
            load_resp.start()
            pl.semaphore_wait(barrier, len(peers))
        for b in batches:
            if sum(BATCHES[b]) == g + 1:
                spread(b)
    begin_chip()

    events = []
    for r in range(-1, FAR):
        if r >= 0:
            events.append((STARTS[0] + r - AHEAD, OWN, functools.partial(step, r=r)))
        events.append((STARTS[0] + r + LAG - AHEAD, OWN, functools.partial(step_across, r=r)))
    for b in batches:
        lead, lead_across = (0.5, 0.3) if b == 0 else LEADS
        events.append((STARTS[b] - lead, b, begin))
        events.append((STARTS[b] - lead_across, b, begin_across))
        for r in range(-1, FAR):
            if r >= 0:
                events.append((STARTS[b] + r, b, functools.partial(step, r=r)))
            events.append((STARTS[b] + r + LAG, b, functools.partial(step_across, r=r)))
        events.append((STARTS[b] + FAR - 1 + LAG, b, finish))
    for _, b, event in sorted(events, key=lambda e: e[:2]):
        event(b)

    for b in batches:
        keep_own(b).wait()
        a_copy(b, me).wait_send()
        for q in range(1, PEERS):
            back_copy(b, q).wait_recv()
            forward_copy(b, q).wait_send()
            back_copy(b, q).wait_send()
    for b in [*batches, OWN]:
        for r in range(-1, FAR):
            for d in ways(r):
                y_copy(d, b, r, y).wait_send()
                for t in range(1 if b == OWN else 3):
                    if r >= 0:
                        z_send(d, t, b, r).wait_send()


def gather(response, focus_plus, table):
    bf16 = jnp.bfloat16
    dma = pltpu.SemaphoreType.DMA
    hbm = pl.BlockSpec(memory_space=pltpu.HBM)
    parts = len(BATCHES) + 1
    return pl.pallas_call(
        gather_kernel,
        out_shape=jax.ShapeDtypeStruct((GROUPS, PEERS, TILE, WIDTH), bf16),
        in_specs=[hbm] * 3,
        out_specs=pl.BlockSpec(memory_space=pl.ANY),
        scratch_shapes=[
            pltpu.VMEM(response.shape, bf16),
            pltpu.VMEM(focus_plus.shape, bf16),
            pltpu.VMEM((HALF, NT), bf16),
            pltpu.VMEM((GROUPS, 2, HALF * FEW, LANES), jnp.float32),
            pltpu.VMEM((GROUPS, PEERS, TILE, WIDTH), bf16),
            pltpu.VMEM((GROUPS, PEERS, TILE, WIDTH), bf16),
            pltpu.VMEM((NJ, 2 * NZ, GROUPS, CHIPS, 2 * PIECE, WIDTH), bf16),
            pltpu.VMEM((NJ, 2, GROUPS * ROWS, WIDTH), jnp.float32),
            pltpu.VMEM((GROUPS, PEERS, TILE, WIDTH), bf16),
            dma((GROUPS + 2,)),
            dma((parts,)),
            dma((parts, PEERS)), dma((parts, PEERS)),
            dma((parts,)), dma((parts,)),
            dma((2, 3, parts, FAR)), dma((2, 3, parts, FAR)),
            dma((2, parts, FAR + 1)), dma((2, parts, FAR + 1)),
            dma((parts, PEERS)), dma((parts, PEERS)),
        ],
        compiler_params=pltpu.CompilerParams(
            collective_id=0, has_side_effects=True, vmem_limit_bytes=63086592
        ),
        name="gather",
    )(response, focus_plus, table)


def inverse_kernel(spectra_ref, table_ref, onset_ref, out_hbm, mine, out, sem):
    times = lax.broadcasted_iota(jnp.int32, (NT, WIDTH), 0)
    waves = table_ref[...]

    def store(i):
        return pltpu.make_async_copy(out.at[i], out_hbm.at[i], sem.at[i])

    for g in range(GROUPS):
        for h in range(2):
            rows = spectra_ref[g, :, :, pl.ds(h * LANES, LANES)].astype(jnp.float32)
            mine[g, h] = rows.reshape(HALF * FEW, LANES)
        for i in range(FEW):
            halves = [mine[g, h, pl.ds(i, HALF, stride=FEW), :] for h in range(2)]
            spectra = jnp.concatenate(halves, axis=1).astype(jnp.bfloat16)
            trace = jnp.dot(waves, spectra, preferred_element_type=jnp.float32)
            at = g * FEW + i
            out[at] = jnp.where(times < onset_ref[at : at + 1, :], trace, 0.0).astype(jnp.bfloat16)
            store(at).start()
    for i in range(FOCAL):
        store(i).wait()


def inverse(spectra, table, onset):
    vmem = pl.BlockSpec(memory_space=pltpu.VMEM)
    shape = (FOCAL, NT, WIDTH)
    return pl.pallas_call(
        inverse_kernel,
        out_shape=jax.ShapeDtypeStruct(shape, jnp.bfloat16),
        in_specs=[vmem] * 3,
        out_specs=pl.BlockSpec(memory_space=pltpu.HBM),
        scratch_shapes=[
            pltpu.VMEM((GROUPS, 2, HALF * FEW, LANES), jnp.float32),
            pltpu.VMEM(shape, jnp.bfloat16),
            pltpu.SemaphoreType.DMA((FOCAL,)),
        ],
        compiler_params=pltpu.CompilerParams(vmem_limit_bytes=8 << 20),
        name="inverse",
    )(spectra, table, onset)


def body(response, focus_plus, onset):
    forward_table, inverse_table = tables()
    spectra = gather(response, focus_plus, jnp.asarray(forward_table))
    return inverse(spectra, jnp.asarray(inverse_table), onset)


def solution(mesh):
    return jax.shard_map(
        body,
        mesh=mesh,
        in_specs=(P(None, "freq", "src", None), P("freq", None, "src"), P("freq", "src")),
        out_specs=P("freq", None, "src"),
        check_vma=False,
    )
```

```python
import functools
import math

import jax
import jax.numpy as jnp
import ml_dtypes
import numpy as np
from jax import lax
from jax.experimental import pallas as pl
from jax.experimental.pallas import tpu as pltpu
from jax.sharding import PartitionSpec as P

MESH = pl.DeviceIdType.MESH

NX = 4
NH = 2
NZ = 8
CHIPS = NX * NH
PEERS = 2 * CHIPS
NJ = 2
FOCAL = 12
GROUPS = 3
FEW = FOCAL // GROUPS
TILE = NJ * 2 * FEW
PIECE = 2 * FEW
ROWS = PEERS * PIECE
HALF = NJ * 2 * PEERS
TABLE = 1024
NT = 256
LANES = 128
SPARE = 8
WIDTH = 256
FAR = NZ // 2
CHIP_PLACES = ((0, 0), (1, 0), (3, 0), (0, 1), (2, 0), (1, 1), (3, 1), (2, 1))
PLACES = tuple((dx, dy, dc) for dx, dy in CHIP_PLACES for dc in range(2))
BATCHES = ((0, 3),)
PLACES_A = (3,)
AHEAD = 1.1
STARTS = (0.0,)
LEADS = (1.5, 0.5)
LAG = 1.05
OWN = len(BATCHES)


def tables():
    samples = np.arange(NT, dtype=np.int32)
    bins = (np.arange(TABLE) // 2 + 1).astype(np.int32)
    part = np.arange(TABLE) % 2
    phase = (bins[:, None] * samples) % NT
    angle = (np.float32(2.0 * math.pi) * phase.astype(np.float32) / np.float32(NT)).astype(np.float32)
    wave = np.where(part[:, None] == 0, np.cos(angle), -np.sin(angle)).astype(np.float32)
    inverse = np.float32(2.0 / NT) * wave[:HALF]
    return wave.astype(ml_dtypes.bfloat16), np.ascontiguousarray(inverse.T).astype(ml_dtypes.bfloat16)


def gather_kernel(
    resp_hbm, focus_hbm, table_hbm, out_hbm,
    resp, focus, table, mine, blocks, arrived, gath, acc, back_out,
    load_sem, own_sem, fwd_s, fwd_r, a_s, a_r, z_s, z_r, y_s, y_r, inv_s, inv_r,
):
    f = lax.axis_index("freq")
    me = lax.axis_index("src")
    core = f % 2
    yh = (f // 2) % 2
    x = f // 4
    y = me // NZ
    z = me % NZ
    partner = (1 - y) * NZ + z
    rings = ((f, y * NZ + (z + 1) % NZ), (f, y * NZ + (z + NZ - 1) % NZ))
    across = (f, partner)

    def device_at(dx, dy, dc):
        return (((x + dx) % NX) * NH + (yh + dy) % NH) * 2 + (core + dc) % 2

    ahead = [device_at(*place) for place in PLACES]
    behind = [device_at(NX - dx, dy, dc) for dx, dy, dc in PLACES]
    batches = range(len(BATCHES))

    def few(ref, g):
        return ref.at[pl.ds(g * FEW, FEW)]

    def load_focus(g):
        return pltpu.make_async_copy(few(focus_hbm, g), few(focus, g), load_sem.at[g])

    load_table = pltpu.make_async_copy(table_hbm.at[pl.ds(0, HALF)], table, load_sem.at[GROUPS])
    load_resp = pltpu.make_async_copy(resp_hbm, resp, load_sem.at[GROUPS + 1])
    load_table.start()
    for g in range(GROUPS):
        load_focus(g).start()
    barrier = pltpu.get_barrier_semaphore()
    peers = [*rings, across] + [(d, me) for d in ahead[1:]]
    for peer in peers:
        pl.semaphore_signal(barrier, inc=1, device_id=peer, device_id_type=MESH)

    def transform(g):
        load_focus(g).wait()
        waves = table[...]

        def one(i, _):
            res = jnp.dot(waves, focus[g * FEW + i], preferred_element_type=jnp.float32)
            for h in range(2):
                mine[g, h, pl.ds(i, HALF, stride=FEW), :] = res[:, h * LANES : (h + 1) * LANES]
            return 0

        lax.fori_loop(0, FEW, one, 0)
        for h in range(2):
            rows = mine[g, h, : HALF * FEW, :].astype(jnp.bfloat16).reshape(PEERS, TILE, LANES)
            blocks[g, :, :, pl.ds(h * LANES, LANES)] = rows

    def groups_of(b):
        return pl.ds(0, GROUPS) if b == OWN else pl.ds(*BATCHES[b])

    def forward_copy(b, q):
        return pltpu.make_async_remote_copy(
            src_ref=blocks.at[groups_of(b), behind[q]], dst_ref=arrived.at[groups_of(b), q],
            send_sem=fwd_s.at[b, q], recv_sem=fwd_r.at[b, q],
            device_id=(behind[q], me), device_id_type=MESH,
        )

    def spread(b):
        for q in range(1, PEERS):
            forward_copy(b, q).start()
        first, count = BATCHES[b]
        for g in range(first, first + count):
            arrived[g, 0] = blocks[g, f]

    def collect(b, first_chip, last_chip):
        for q in range(2 * first_chip, 2 * last_chip):
            if q > 0:
                forward_copy(b, q).wait_recv()
        first, count = BATCHES[b]
        for g in range(first, first + count):
            for p in range(first_chip, last_chip):
                both = [arrived[g, 2 * p + c].astype(jnp.float32) for c in range(2)]
                for j in range(NJ):
                    rows = [tile[j * PIECE : (j + 1) * PIECE] for tile in both]
                    gath[j, me, g, p] = jnp.concatenate(rows, axis=0).astype(jnp.bfloat16)

    def span(b, t):
        if b == OWN:
            return pl.ds(0, 1)
        return pl.ds(1, PLACES_A[b]) if t else pl.ds(1 + PLACES_A[b], CHIPS - 1 - PLACES_A[b])

    def owner(d, r, column):
        return column * NZ + ((z + 2 * NZ - 1 - r) % NZ if d == 0 else (z + 1 + r) % NZ)

    def piece(b, d, r, o, places):
        if r < FAR - 1:
            return gath.at[:, o, groups_of(b), places]
        return gath.at[d, o, groups_of(b), places]

    def z_copy(d, t, b, r, o):
        block = piece(b, d, r, o, span(b, t))
        return pltpu.make_async_remote_copy(
            src_ref=block, dst_ref=block, send_sem=z_s.at[d, t, b, r], recv_sem=z_r.at[d, t, b, r],
            device_id=rings[d], device_id_type=MESH,
        )

    def z_send(d, t, b, r):
        return z_copy(d, t, b, r, owner(d, r - 1, 1 - y if t == 2 else y))

    def z_recv(d, t, b, r):
        return z_copy(d, t, b, r, owner(d, r, 1 - y if t == 2 else y))

    def y_copy(d, b, r, column):
        block = piece(b, d, r, owner(d, r, column), span(b, 0))
        return pltpu.make_async_remote_copy(
            src_ref=block, dst_ref=block, send_sem=y_s.at[d, b, r + 1], recv_sem=y_r.at[d, b, r + 1],
            device_id=across, device_id_type=MESH,
        )

    def a_copy(b, o):
        block = piece(b, 0, -1, o, span(b, 1))
        return pltpu.make_async_remote_copy(
            src_ref=block, dst_ref=block, send_sem=a_s.at[b], recv_sem=a_r.at[b],
            device_id=across, device_id_type=MESH,
        )

    def ways(r):
        return (0,) if r < 0 else (0, 1)

    def products(b, owners, fresh=False):
        first, count = BATCHES[b]
        rows = pl.ds(first * ROWS, count * ROWS)

        def one(d, _):
            for c in range(2):
                total = None
                for o in owners:
                    columns = pl.ds(pl.multiple_of(o * WIDTH, WIDTH), WIDTH)
                    block = gath[d, o, pl.ds(first, count)].reshape(count * ROWS, WIDTH)
                    term = lax.dot_general(
                        block, resp[c, d, :, columns], (((1,), (1,)), ((), ())),
                        preferred_element_type=jnp.float32,
                    )
                    total = term if total is None else total + term
                if fresh:
                    acc[d, c, rows, :] = total
                else:
                    acc[d, c, rows, :] += total
            return 0

        lax.fori_loop(0, NJ, one, 0)

    def begin_chip():
        for b in batches:
            collect(b, 0, 1)
        for d in range(2):
            z_send(d, 0, OWN, 0).start()
        y_copy(0, OWN, -1, y).start()

    def begin(b):
        collect(b, 1, 1 + PLACES_A[b])
        a_copy(b, me).start()
        for d in range(2):
            z_send(d, 1, b, 0).start()
        collect(b, 1 + PLACES_A[b], CHIPS)
        for d in range(2):
            z_send(d, 0, b, 0).start()
        y_copy(0, b, -1, y).start()

    def begin_across(b):
        if b == 0:
            load_resp.wait()
        a_copy(b, partner).wait_recv()
        for d in range(2):
            z_send(d, 2, b, 0).start()
        products(b, [me], fresh=True)

    def owners_at(r, column):
        both = [owner(d, r, column) for d in ways(r)]
        return [partner] if r < 0 else both[:1] if r == FAR - 1 else both

    def step(b, r):
        for t in range(1 if b == OWN else 3):
            for d in range(2):
                z_recv(d, t, b, r).wait_recv()
                if r < FAR - 1:
                    z_send(d, t, b, r + 1).start()
                if t == 0:
                    y_copy(d, b, r, y).start()
        if b != OWN:
            products(b, owners_at(r, y))

    def step_across(b, r):
        for d in ways(r):
            y_copy(d, b, r, 1 - y).wait_recv()
        if b != OWN:
            products(b, owners_at(r, 1 - y))

    def back_copy(b, q):
        return pltpu.make_async_remote_copy(
            src_ref=back_out.at[groups_of(b), q], dst_ref=out_hbm.at[groups_of(b), f],
            send_sem=inv_s.at[b, q], recv_sem=inv_r.at[b, q],
            device_id=(ahead[q], me), device_id_type=MESH,
        )

    def keep_own(b):
        return pltpu.make_async_copy(back_out.at[groups_of(b), 0], out_hbm.at[groups_of(b), f], own_sem.at[b])

    def finish(b):
        sign = jnp.where(lax.broadcasted_iota(jnp.int32, (PIECE, WIDTH), 0) < FEW, -1.0, 1.0)
        first, count = BATCHES[b]
        for q in range(PEERS - 1, -1, -1):
            for g in range(first, first + count):
                rows = pl.ds(g * ROWS + q * PIECE, PIECE)
                bins = [
                    acc[j, 0, rows, :] + sign * pltpu.roll(acc[j, 1, rows, :], FEW, 0) for j in range(NJ)
                ]
                back_out[g, q] = jnp.concatenate(bins, axis=0).astype(jnp.bfloat16)
            if q > 0:
                back_copy(b, q).start()
            else:
                keep_own(b).start()

    load_table.wait()
    for g in range(GROUPS):
        transform(g)
        if g == 0:
            load_resp.start()
            pl.semaphore_wait(barrier, len(peers))
        for b in batches:
            if sum(BATCHES[b]) == g + 1:
                spread(b)
    begin_chip()

    events = []
    for r in range(-1, FAR):
        if r >= 0:
            events.append((STARTS[0] + r - AHEAD, OWN, functools.partial(step, r=r)))
        events.append((STARTS[0] + r + LAG - AHEAD, OWN, functools.partial(step_across, r=r)))
    for b in batches:
        lead, lead_across = (0.5, 0.3) if b == 0 else LEADS
        events.append((STARTS[b] - lead, b, begin))
        events.append((STARTS[b] - lead_across, b, begin_across))
        for r in range(-1, FAR):
            if r >= 0:
                events.append((STARTS[b] + r, b, functools.partial(step, r=r)))
            events.append((STARTS[b] + r + LAG, b, functools.partial(step_across, r=r)))
        events.append((STARTS[b] + FAR - 1 + LAG, b, finish))
    for _, b, event in sorted(events, key=lambda e: e[:2]):
        event(b)

    for b in batches:
        keep_own(b).wait()
        a_copy(b, me).wait_send()
        for q in range(1, PEERS):
            back_copy(b, q).wait_recv()
            forward_copy(b, q).wait_send()
            back_copy(b, q).wait_send()
    for b in [*batches, OWN]:
        for r in range(-1, FAR):
            for d in ways(r):
                y_copy(d, b, r, y).wait_send()
                for t in range(1 if b == OWN else 3):
                    if r >= 0:
                        z_send(d, t, b, r).wait_send()


def gather(response, focus_plus, table):
    bf16 = jnp.bfloat16
    dma = pltpu.SemaphoreType.DMA
    hbm = pl.BlockSpec(memory_space=pltpu.HBM)
    parts = len(BATCHES) + 1
    return pl.pallas_call(
        gather_kernel,
        out_shape=jax.ShapeDtypeStruct((GROUPS, PEERS, TILE, WIDTH), bf16),
        in_specs=[hbm] * 3,
        out_specs=pl.BlockSpec(memory_space=pl.ANY),
        scratch_shapes=[
            pltpu.VMEM(response.shape, bf16),
            pltpu.VMEM(focus_plus.shape, bf16),
            pltpu.VMEM((HALF, NT), bf16),
            pltpu.VMEM((GROUPS, 2, HALF * FEW + SPARE, LANES), jnp.float32),
            pltpu.VMEM((GROUPS, PEERS, TILE, WIDTH), bf16),
            pltpu.VMEM((GROUPS, PEERS, TILE, WIDTH), bf16),
            pltpu.VMEM((NJ, 2 * NZ, GROUPS, CHIPS, 2 * PIECE, WIDTH), bf16),
            pltpu.VMEM((NJ, 2, GROUPS * ROWS, WIDTH), jnp.float32),
            pltpu.VMEM((GROUPS, PEERS, TILE, WIDTH), bf16),
            dma((GROUPS + 2,)),
            dma((parts,)),
            dma((parts, PEERS)), dma((parts, PEERS)),
            dma((parts,)), dma((parts,)),
            dma((2, 3, parts, FAR)), dma((2, 3, parts, FAR)),
            dma((2, parts, FAR + 1)), dma((2, parts, FAR + 1)),
            dma((parts, PEERS)), dma((parts, PEERS)),
        ],
        compiler_params=pltpu.CompilerParams(
            collective_id=0, has_side_effects=True, vmem_limit_bytes=63086592
        ),
        name="gather",
    )(response, focus_plus, table)


def inverse_kernel(spectra_ref, table_ref, onset_ref, out_hbm, mine, out, sem):
    times = lax.broadcasted_iota(jnp.int32, (NT, WIDTH), 0)
    waves = table_ref[...]

    def store(i):
        return pltpu.make_async_copy(out.at[i], out_hbm.at[i], sem.at[i])

    for g in range(GROUPS):
        for h in range(2):
            rows = spectra_ref[g, :, :, pl.ds(h * LANES, LANES)].astype(jnp.float32)
            mine[g, h, : HALF * FEW, :] = rows.reshape(HALF * FEW, LANES)
        for i in range(FEW):
            halves = [mine[g, h, pl.ds(i, HALF, stride=FEW), :] for h in range(2)]
            spectra = jnp.concatenate(halves, axis=1).astype(jnp.bfloat16)
            trace = jnp.dot(waves, spectra, preferred_element_type=jnp.float32)
            at = g * FEW + i
            out[at] = jnp.where(times < onset_ref[at : at + 1, :], trace, 0.0).astype(jnp.bfloat16)
            store(at).start()
    for i in range(FOCAL):
        store(i).wait()


def inverse(spectra, table, onset):
    vmem = pl.BlockSpec(memory_space=pltpu.VMEM)
    shape = (FOCAL, NT, WIDTH)
    return pl.pallas_call(
        inverse_kernel,
        out_shape=jax.ShapeDtypeStruct(shape, jnp.bfloat16),
        in_specs=[vmem] * 3,
        out_specs=pl.BlockSpec(memory_space=pltpu.HBM),
        scratch_shapes=[
            pltpu.VMEM((GROUPS, 2, HALF * FEW + SPARE, LANES), jnp.float32),
            pltpu.VMEM(shape, jnp.bfloat16),
            pltpu.SemaphoreType.DMA((FOCAL,)),
        ],
        compiler_params=pltpu.CompilerParams(vmem_limit_bytes=8 << 20),
        name="inverse",
    )(spectra, table, onset)


def body(response, focus_plus, onset):
    forward_table, inverse_table = tables()
    spectra = gather(response, focus_plus, jnp.asarray(forward_table))
    return inverse(spectra, jnp.asarray(inverse_table), onset)


def solution(mesh):
    return jax.shard_map(
        body,
        mesh=mesh,
        in_specs=(P(None, "freq", "src", None), P("freq", None, "src"), P("freq", "src")),
        out_specs=P("freq", None, "src"),
        check_vma=False,
    )
```
